32 devices in a mesh: rep: 2 (over x), shard: 16 (over z, y, core).
Axes of the slice: x: 2, y: 2, z: 4, core: 2. Of those that a mesh axis runs over, the one named last changes fastest.
Arguments:
- tokens: bfloat16 [4096, 768], P(('rep', 'shard')), may hold values from -6 to 6
- cotangent: bfloat16 [4096, 768], P(('rep', 'shard')), may hold values from -6 to 6
- lengths: int32 [32, 3], P(('rep', 'shard')), may hold values from 1 to 96, 128 in all within a row
- routes: int32 [4096, 1], P(('rep', 'shard')), may hold values from 0 to 1; in each aligned block of 128 rows (0 to 127, 128 to 255, ...) at most 80 rows name the same one
- bucket_ids: int32 [255], replicated, may hold values from 0 to 31
- attn_in: bfloat16 [3, 768, 768], P(None, 'shard'), may hold values from -0.21875 to 0.21875
- attn_out: bfloat16 [768, 768], P('shard'), may hold values from -0.875 to 0.875
- gains: bfloat16 [2, 768], P(None, 'shard'), may hold values from 0.25 to 1.75
- router: bfloat16 [768, 2], P('shard'), may hold values from -0.109375 to 0.109375
- rel_table: bfloat16 [32, 12], P('shard'), may hold values from -4 to 4
- expert_in: bfloat16 [2, 768, 3072], P(None, 'shard'), may hold values from -0.21875 to 0.21875
- expert_out: bfloat16 [2, 3072, 768], P(None, 'shard'), may hold values from -0.21875 to 0.21875
Outputs:
- layer_out: bfloat16 [4096, 768], P(('rep', 'shard'))
- input_grad: float32 [4096, 768], P(('rep', 'shard'))
- grad_attn_in: float32 [3, 768, 768], P(None, 'shard')
- grad_attn_out: float32 [768, 768], P('shard')
- grad_gains: float32 [2, 768], P(None, 'shard')
- grad_router: float32 [768, 2], P('shard')
- grad_rel_table: float32 [32, 12], P('shard')
- grad_expert_in: float32 [2, 768, 3072], P(None, 'shard')
- grad_expert_out: float32 [2, 3072, 768], P(None, 'shard')
The draws below stay inside these ranges and needn't reach their ends.
Inputs may be any that keep to these rules, and one draw needn't show every extreme that they name: Row b holds the lengths of the 3 sequences of device block b; they sum to 128, and some block has one of exactly 96. `routes`: within the 128 rows of one device no expert is named more than 80 times, and in every draw some device names some expert exactly 80 times.
All inputs are finite; a program needn't handle non-finite values.
Results may differ from the reference program's by a relative error of at most 0.012.
Values may be sent and summed in bfloat16 or wider, within the bound.
A program may use at most 192 MiB of HBM per device.

```python
import math
import jax
import jax.numpy as jnp
import numpy as np
from jax import lax

D = 768
H = 12
HD = 64
FF = 3072
BUCKETS = 32
E = 2
SEQ_DEV = 3
TOK_DEV = 128
CAP = 80
MAX_LEN = 96
BLOCKS = 32
TOKENS = 4096


def place_ends(entries, stream_key, least, high):
    extent = entries.shape
    spot = [jax.random.randint(jax.random.fold_in(stream_key, axis), (), 0, extent[axis]) for axis in range(len(extent))]
    entries = entries.at[tuple(spot)].set(least)
    longest = extent.index(max(extent))
    spot[longest] = (spot[longest] + 1) % extent[longest]
    return entries.at[tuple(spot)].set(high)


def level_of(own_key, extent, pieces, smallest, top_value):
    factor_of, own = 1.0, jax.random.fold_in(own_key, 6)
    for position, shards_of in pieces:
        steps = jnp.exp(jax.random.uniform(jax.random.fold_in(own, position), (shards_of,), jnp.float32, smallest / len(pieces), top_value / len(pieces)))
        factor_of = factor_of * jnp.repeat(steps, extent[position] // shards_of).reshape([-1 if axis == position else 1 for axis in range(len(extent))])
    return factor_of


def profile(amount, total, most, slope):
    loads = [(1 << 20) // math.isqrt(rank ** slope) + 1 for rank in range(2, amount + 1)]
    rest, counts = total - most - (amount - 1), [1] * (amount - 1)
    while rest > 0:
        candidates = [i for i in range(amount - 1) if counts[i] < most]
        whole, remaining = sum([loads[i] for i in candidates]), rest
        for i in candidates:
            extra = min(most - counts[i], max(1, remaining * loads[i] // whole), rest)
            counts[i] = counts[i] + extra
            rest = rest - extra
    return np.array([most] + counts)


def ragged_sizes(key, count, total, limit, lean):
    if count == 2:
        one = jax.random.randint(key, (), max(1, total - limit), min(limit, total - 1) + 1)
        return jnp.stack([one, total - one])
    sizes = jnp.asarray(profile(count, total, limit, lean), jnp.int32)
    pairs = (count - 1) // 2
    giver, receiver = sizes[1:1 + 2 * pairs:2], sizes[2:2 + 2 * pairs:2]
    room = jnp.minimum(giver - 1, limit - receiver)
    shifted = jax.random.randint(jax.random.fold_in(key, 1), (pairs,), 0, 1 << 20) % (room + 1)
    sizes = sizes.at[1:1 + 2 * pairs:2].set(giver - shifted).at[2:2 + 2 * pairs:2].set(receiver + shifted)
    return sizes[jax.random.permutation(jax.random.fold_in(key, 2), count)]


def deal_out(key, own, number, rows, count, top, most, slope):
    sequence = jax.random.permutation(key, count)
    packed, ordinary = portions_of(count, rows * top, most, slope, True), portions_of(count, rows * top, most, slope, False)
    places = jnp.arange(count)

    def named(sizes, turn):
        used = int((sizes > 0).sum())
        fixed = max(1, used // 4)
        moved = fixed + (places - fixed + turn * (used - fixed)) % max(1, count - fixed)
        return jnp.zeros((count,), jnp.int32).at[sequence[jnp.where(places < fixed, places, moved)]].set(jnp.asarray(sizes, jnp.int32))

    sizes = jnp.where(number % 4 == 0, named(packed, number // 4), named(ordinary, number - number // 4 - 1))
    mixed = jax.random.permutation(jax.random.fold_in(own, 3), count)
    giver, taker = mixed[0:count // 2 * 2:2], mixed[1:count // 2 * 2:2]
    slack = jnp.minimum(sizes[giver] - 1, most - sizes[taker]) // 2
    slack = jnp.where((giver == sequence[0]) | (taker == sequence[0]) | (sizes[taker] == 0), 0, jnp.maximum(slack, 0))
    moved = jax.random.randint(jax.random.fold_in(own, 4), (count // 2,), 0, 1 << 20) % (slack + 1)
    sizes = sizes.at[giver].add(-moved).at[taker].add(moved)
    labels = jnp.searchsorted(jnp.cumsum(sizes), jnp.arange(rows * top), side="right").astype(jnp.int32)
    listing = labels.reshape(top, rows).T
    listing = listing[jax.random.permutation(jax.random.fold_in(own, 1), rows)]
    turn = jax.random.randint(jax.random.fold_in(own, 2), (rows, 1), 0, top)
    return jnp.take_along_axis(listing, (jnp.arange(top)[None, :] + turn) % top, axis=1)


def portions_of(number_of, total, bound, lean, full):
    weights = [(1 << 20) // math.isqrt(grade ** lean) + 1 for grade in range(1, number_of + 1)]
    largest = bound if full else min(bound, max(-(-total // number_of), total * weights[0] // sum(weights)))
    least = 1 if total - largest >= number_of - 1 else 0
    holding, rest = [largest] + [least] * (number_of - 1), total - largest - least * (number_of - 1)
    while rest > 0:
        movable = [i for i in range(1, number_of) if holding[i] < largest] or [i for i in range(1, number_of) if holding[i] < bound]
        pool, remaining = sum([weights[i] for i in movable]), rest
        for i in movable:
            addition = min(bound - holding[i], max(1, remaining * weights[i] // pool), rest)
            holding[i] = holding[i] + addition
            rest = rest - addition
    return np.array(holding)


def normal_values(stream_key, shape, scale, limit, cuts=(), kind=jnp.bfloat16):
    level = level_of(stream_key, shape, cuts, -0.22, 0.18) if cuts else 1.0
    values = jax.random.normal(stream_key, shape, jnp.float32) * scale * level
    return jnp.minimum(jnp.maximum(values, -limit), limit).astype(kind)


def setup_inputs(seed: int = 0) -> dict:
    key_list = jax.random.split(jax.random.key(seed), 13)
    tokens = normal_values(key_list[0], (TOKENS, D), 1.0, 6.0, ((0, 32),))
    cotangent = normal_values(key_list[1], (TOKENS, D), 1.0, 6.0, ((0, 32),))
    lengths = jax.vmap(lambda own: ragged_sizes(own, SEQ_DEV, TOK_DEV, MAX_LEN, 2))(jax.random.split(key_list[2], BLOCKS)).reshape((BLOCKS, SEQ_DEV)).astype(jnp.int32)
    routes_keys = jax.random.split(jax.random.fold_in(key_list[3], 1), TOKENS // TOK_DEV)
    routes_turns = jax.random.permutation(jax.random.fold_in(key_list[3], 3), TOKENS // TOK_DEV)
    routes = jax.vmap(lambda own, number: deal_out(jax.random.fold_in(key_list[3], 2), own, number, TOK_DEV, E, 1, CAP, 1))(routes_keys, routes_turns).reshape((TOKENS, 1))
    bucket_ids = place_ends(jax.random.randint(key_list[4], (2 * TOK_DEV - 1,), 0, BUCKETS), jax.random.fold_in(key_list[4], 1), 0, BUCKETS - 1).astype(jnp.int32)
    attn_in = normal_values(key_list[5], (3, D, D), D ** -0.5, 0.21875, ((1, 16),))
    attn_out = normal_values(key_list[6], (D, D), (D // 16) ** -0.5, 0.875, ((0, 16),))
    gains = jnp.clip(1.0 + 0.15 * jax.random.normal(key_list[7], (2, D), jnp.float32), 0.25, 1.75).astype(jnp.bfloat16)
    router = normal_values(key_list[8], (D, E), (4 * D) ** -0.5, 0.109375, ((0, 16),))
    rel_table = normal_values(key_list[9], (BUCKETS, H), 1.0, 4.0, ((0, 16),))
    expert_in = normal_values(key_list[10], (E, D, FF), D ** -0.5, 0.21875, ((1, 16),))
    expert_out = normal_values(key_list[11], (E, FF, D), (FF // 4) ** -0.5, 0.21875, ((1, 16),))
    return {"tokens": tokens, "cotangent": cotangent, "lengths": lengths, "routes": routes, "bucket_ids": bucket_ids, "attn_in": attn_in, "attn_out": attn_out, "gains": gains, "router": router, "rel_table": rel_table, "expert_in": expert_in, "expert_out": expert_out}


@jax.custom_vjp
def low(v):
    return lax.optimization_barrier(v.astype(jnp.bfloat16)).astype(jnp.float32)

@jax.custom_vjp
def low_back(v):
    return v

def low_keep(v):
    return (low(v), None)

def low_pass(kept, grad):
    return (grad,)

def back_keep(v):
    return (v, None)

def back_low(kept, grad):
    return (low(grad),)
low.defvjp(low_keep, low_pass)
low_back.defvjp(back_keep, back_low)

def rms_norm(values, gain):
    return values * lax.rsqrt(lax.optimization_barrier(jnp.mean(values * values, axis=-1, keepdims=True)) + 1e-06) * gain

def block_layer(params, tokens, lengths, routes, bucket_ids):
    attn_in, attn_out, gains, router, rel_table, expert_in, expert_out = params
    highest = lax.Precision.HIGHEST
    rows = tokens.shape[0]
    normed = low(rms_norm(tokens, gains[0]))
    projected = low(low_back(jnp.einsum('td,kde->kte', normed, attn_in, precision=highest)))
    query = projected[0].reshape(rows, H, HD)
    keys = projected[1].reshape(rows, H, HD)
    values = projected[2].reshape(rows, H, HD)
    raw = low_back(jnp.einsum('qhc,khc->hqk', query, keys, precision=highest) * 0.125)
    places = jnp.arange(rows, dtype=jnp.int32)
    offsets = places[None, :] - places[:, None] + (rows - 1)
    buckets = jnp.take(bucket_ids, offsets, axis=0)
    bias = jnp.transpose(jnp.take(rel_table, buckets, axis=0), (2, 0, 1))
    ends = jnp.cumsum(lengths)
    segment = lax.optimization_barrier(jnp.sum((places[:, None] >= ends[None, :]).astype(jnp.int32), axis=1))
    allowed = segment[:, None] == segment[None, :]
    scores = jnp.where(allowed[None], raw + bias, -1e+30)
    peak = lax.optimization_barrier(jnp.max(scores, axis=-1, keepdims=True))
    expo = jnp.exp(scores - peak)
    probs = low(expo / lax.optimization_barrier(jnp.sum(expo, axis=-1, keepdims=True)))
    context = low(low_back(jnp.einsum('hqk,khc->qhc', probs, values, precision=highest))).reshape(rows, D)
    hidden = tokens + low_back(jnp.dot(context, attn_out, precision=highest))
    normed_ffn = low(rms_norm(hidden, gains[1]))
    logits = jnp.dot(normed_ffn, router, precision=highest)
    gate_probs = jax.nn.softmax(logits, axis=-1)
    chosen = routes[:, 0]
    picked = chosen[:, None] == jnp.arange(E, dtype=jnp.int32)[None, :]
    gate = lax.optimization_barrier(jnp.sum(jnp.where(picked, gate_probs, 0.0), axis=1))
    ranks = jnp.cumsum(picked.astype(jnp.int32), axis=0) - 1
    slot = chosen * CAP + lax.optimization_barrier(jnp.sum(jnp.where(picked, ranks, 0), axis=1))
    dispatch = (jnp.arange(E * CAP, dtype=jnp.int32)[:, None] == slot[None, :]).astype(jnp.float32)
    buffers = jnp.dot(dispatch, normed_ffn, precision=highest).reshape(E, CAP, D)
    before = low_back(jnp.einsum('ecd,edf->ecf', buffers, expert_in, precision=highest))
    active = low(jax.nn.gelu(before, approximate=True))
    returned = low_back(jnp.einsum('ecf,efd->ecd', active, expert_out, precision=highest)).reshape(E * CAP, D)
    gathered = jnp.take(returned, slot, axis=0)
    return hidden + gate[:, None] * gathered

def reference(tokens, cotangent, lengths, routes, bucket_ids, attn_in, attn_out, gains, router, rel_table, expert_in, expert_out):
    params = (attn_in.astype(jnp.float32), attn_out.astype(jnp.float32), gains.astype(jnp.float32), router.astype(jnp.float32), rel_table.astype(jnp.float32), expert_in.astype(jnp.float32), expert_out.astype(jnp.float32))
    token_blocks = tokens.astype(jnp.float32).reshape(BLOCKS, TOK_DEV, D)
    route_blocks = routes.reshape(BLOCKS, TOK_DEV, 1)

    def forward(weights, inputs):

        def single(items):
            return block_layer(weights, items[0], items[1], items[2], bucket_ids)
        return lax.map(jax.checkpoint(single), (inputs, lengths, route_blocks))
    result, pullback = jax.vjp(forward, params, token_blocks)
    param_grads, token_grads = pullback(cotangent.astype(jnp.float32).reshape(BLOCKS, TOK_DEV, D))
    return (result.reshape(TOKENS, D).astype(jnp.bfloat16), token_grads.reshape(TOKENS, D), param_grads[0], param_grads[1], param_grads[2], param_grads[3], param_grads[4], param_grads[5], param_grads[6])
```

```python
import functools

import jax
import jax.numpy as jnp
from jax import lax
from jax.sharding import PartitionSpec as P

BUCKETS = 32
CAP = 80


epsilon = 1e-06


def rms_norm(values, gain):
    return values * lax.rsqrt(jnp.mean(values * values, axis=-1, keepdims=True) + epsilon) * gain


def gelu_tanh(values):
    return jax.nn.gelu(values, approximate=True)


def offsets_to_pairs(per_offset, length):
    heads = per_offset.shape[0]
    reverse = per_offset[:, ::-1]
    repeated = jnp.broadcast_to(reverse[:, None, :], (heads, length, 2 * length - 1))
    repeated = repeated.reshape(heads, length * (2 * length - 1))
    repeated = jnp.pad(repeated, ((0, 0), (0, length)))
    skewed = repeated.reshape(heads, length, 2 * length)[:, :, :length]
    return skewed[:, :, ::-1]


def pairs_to_offsets(grid, length):
    heads = grid.shape[0]
    flipped = grid[:, :, ::-1]
    padded = jnp.pad(flipped, ((0, 0), (0, 0), (0, length)))
    flat = padded.reshape(heads, 2 * length * length)[:, : length * (2 * length - 1)]
    skewed = flat.reshape(heads, length, 2 * length - 1)
    return jnp.sum(skewed, axis=1)[:, ::-1]


def swap(array, size):
    return lax.ppermute(array, "shard", [(i, i ^ 1) for i in range(size)])


def pair_order(core, mine, other, axis):
    first = jnp.where(core == 0, mine, other)
    second = jnp.where(core == 0, other, mine)
    return jnp.concatenate([first, second], axis=axis)


def rep_sum(array, reps):
    if reps == 2:
        other = lax.ppermute(array, "rep", [(0, 1), (1, 0)])
        return array.astype(jnp.float32) + other.astype(jnp.float32)
    return lax.psum(array.astype(jnp.float32), "rep")


def pick(array, index, axis=0):
    return lax.dynamic_index_in_dim(array, index, axis, keepdims=False)


def pad_row(values, width):
    flat = values.reshape(-1)
    return jnp.pad(flat, (0, width - flat.shape[0])).reshape(1, width)


def shards(
    size,
    reps,
    tokens,
    cotangent,
    lengths,
    routes,
    bucket_ids,
    attn_in,
    attn_out,
    gains,
    router,
    rel_table,
    expert_in,
    expert_out,
):
    highest = lax.Precision.HIGHEST
    low = jnp.bfloat16
    length, width = tokens.shape
    heads = rel_table.shape[1]
    head_size = width // heads
    experts = expert_in.shape[0]
    capacity = CAP
    bucket_count = BUCKETS
    chips = size // 2
    rows = width // size
    hidden_units = expert_in.shape[2]
    strip = hidden_units // chips
    groups = [[2 * j + c for j in range(chips)] for c in range(2)]
    core = lax.axis_index("shard") % 2

    packed = jnp.concatenate(
        [
            attn_in.reshape(3 * rows, width),
            attn_out,
            pad_row(gains, width),
            pad_row(router, width),
            pad_row(rel_table, width),
        ],
        axis=0,
    )
    depth = packed.shape[0]
    extra = -depth % 16
    packed = jnp.pad(packed, ((0, extra), (0, 0)))
    depth = depth + extra
    same = lax.all_gather(packed, "shard", axis=0, tiled=False, axis_index_groups=groups)
    other = swap(same, size)
    whole = jnp.stack(
        [jnp.where(core == 0, same, other), jnp.where(core == 0, other, same)], axis=1
    ).reshape(size, depth, width)
    full_in = whole[:, : 3 * rows].reshape(size, 3, rows, width)
    full_in = jnp.transpose(full_in, (1, 0, 2, 3)).reshape(3, width, width)
    full_out = whole[:, 3 * rows : 4 * rows].reshape(width, width)
    spot = 4 * rows
    full_gains = whole[:, spot, : 2 * rows].reshape(size, 2, rows)
    full_gains = jnp.transpose(full_gains, (1, 0, 2)).reshape(2, width)
    full_router = whole[:, spot + 1, : experts * rows].reshape(width, experts)
    table_rows = bucket_count // size
    full_table = whole[:, spot + 2, : table_rows * heads].reshape(bucket_count, heads)

    in_mine = pick(expert_in, core)
    in_other = swap(pick(expert_in, 1 - core), size)
    in_rows = pair_order(core, in_mine, in_other, 0).reshape(2 * rows, chips, strip)
    in_rows = jnp.transpose(in_rows, (1, 0, 2))
    in_strip = lax.all_to_all(
        in_rows, "shard", 0, 0, axis_index_groups=groups, tiled=True
    ).reshape(width, strip)
    out_mine = pick(expert_out, core)
    out_other = swap(pick(expert_out, 1 - core), size)
    out_strip = pair_order(core, out_mine, out_other, 0)

    inputs = tokens.astype(jnp.float32)
    upstream = cotangent.astype(jnp.float32)
    gain_attn = full_gains[0].astype(jnp.float32)
    gain_ffn = full_gains[1].astype(jnp.float32)
    normed = rms_norm(inputs, gain_attn).astype(low)
    projected = jnp.einsum(
        "td,kde->kte", normed, full_in, preferred_element_type=jnp.float32
    ).astype(low)
    query = projected[0].reshape(length, heads, head_size)
    keys = projected[1].reshape(length, heads, head_size)
    values = projected[2].reshape(length, heads, head_size)
    places = jnp.arange(length, dtype=jnp.int32)
    offset_onehot = (
        bucket_ids[:, None] == jnp.arange(bucket_count, dtype=jnp.int32)[None, :]
    ).astype(jnp.float32)
    offset_bias = jnp.einsum(
        "ob,bh->ho", offset_onehot, full_table.astype(jnp.float32), precision=highest
    )
    bias = offsets_to_pairs(offset_bias, length)
    seqs = jnp.arange(lengths.shape[1], dtype=jnp.int32)
    ends = jnp.sum(jnp.where(seqs[None, :] <= seqs[:, None], lengths[0][None, :], 0), axis=1)
    segment = jnp.sum((places[:, None] >= ends[None, :]).astype(jnp.int32), axis=1)
    allowed = segment[:, None] == segment[None, :]
    raw = jnp.einsum("qhc,khc->hqk", query, keys, preferred_element_type=jnp.float32) * 0.125
    scores = jnp.where(allowed[None], raw + bias, -1e30)
    peak = jnp.max(scores, axis=-1, keepdims=True)
    expo = jnp.exp(scores - peak)
    totals = jnp.sum(expo, axis=-1, keepdims=True)
    probs = expo / totals
    probs_low = probs.astype(low)
    context = jnp.einsum("hqk,khc->qhc", probs_low, values, preferred_element_type=jnp.float32)
    context = context.astype(low).reshape(length, width)
    hidden = inputs + jnp.dot(context, full_out, preferred_element_type=jnp.float32)
    normed_ffn = rms_norm(hidden, gain_ffn).astype(low)
    logits = jnp.dot(normed_ffn, full_router, preferred_element_type=jnp.float32)
    gate_probs = jax.nn.softmax(logits, axis=-1)
    chosen = routes[:, 0]
    picked = chosen[:, None] == jnp.arange(experts, dtype=jnp.int32)[None, :]
    gate = jnp.sum(jnp.where(picked, gate_probs, 0.0), axis=1)
    earlier = (places[None, :] < places[:, None]).astype(low)
    ranks = jnp.dot(earlier, picked.astype(low), preferred_element_type=jnp.float32)
    rank = jnp.sum(jnp.where(picked, ranks, 0.0), axis=1).astype(jnp.int32)
    slot = chosen * capacity + rank
    dispatch = (jnp.arange(experts * capacity, dtype=jnp.int32)[:, None] == slot[None, :]).astype(
        low
    )
    scaled = (gate[:, None] * upstream).astype(low)
    both = jnp.concatenate([normed_ffn, scaled], axis=1)
    sent = jnp.dot(dispatch, both, preferred_element_type=jnp.float32).astype(low)
    sent = sent.reshape(experts, capacity, 2 * width)
    sent_mine = pick(sent, core)
    sent_other = swap(pick(sent, 1 - core), size)
    block = jnp.concatenate([sent_mine, sent_other], axis=0)
    arrived = lax.all_gather(block, "shard", axis=0, tiled=True, axis_index_groups=groups)
    batch = arrived[:, :width]
    out_grad = arrived[:, width:]
    before = jnp.dot(batch, in_strip, preferred_element_type=jnp.float32)
    active_wide, pull = jax.vjp(gelu_tanh, before)
    active = active_wide.astype(low)
    returned = jnp.dot(active, out_strip, preferred_element_type=jnp.float32)
    active_grad = jnp.einsum("cd,fd->cf", out_grad, out_strip, preferred_element_type=jnp.float32)
    before_grad = pull(active_grad)[0].astype(low)
    batch_grad = jnp.einsum("cf,df->cd", before_grad, in_strip, preferred_element_type=jnp.float32)
    partial = jnp.concatenate([returned.astype(low), batch_grad.astype(low)], axis=1)
    summed = lax.psum_scatter(
        partial, "shard", scatter_dimension=0, tiled=True, axis_index_groups=groups
    )
    back_mine = summed[:capacity]
    back_other = swap(summed[capacity:], size)
    back = pair_order(core, back_mine, back_other, 0)

    in_grad = jnp.einsum("cd,cf->df", batch, before_grad, preferred_element_type=jnp.float32)
    outer_grad = jnp.einsum("cf,cd->fd", active, out_grad, preferred_element_type=jnp.float32)
    in_grad = lax.all_to_all(
        in_grad.astype(low).reshape(chips, 2 * rows, strip),
        "shard",
        0,
        0,
        axis_index_groups=groups,
        tiled=True,
    )
    in_grad = rep_sum(in_grad, reps)
    in_grad = jnp.transpose(in_grad, (1, 0, 2)).reshape(2, rows, hidden_units)
    grad_mine = pick(in_grad, core)
    grad_other = swap(pick(in_grad, 1 - core).astype(low), size).astype(jnp.float32)
    expert_in_grad = pair_order(core, grad_mine[None], grad_other[None], 0)
    outer_grad = rep_sum(outer_grad.astype(low), reps).reshape(2, strip // 2, width)
    outer_mine = pick(outer_grad, core)
    outer_other = swap(pick(outer_grad, 1 - core).astype(low), size).astype(jnp.float32)
    expert_out_grad = pair_order(core, outer_mine[None], outer_other[None], 0)

    gathered_all = jnp.einsum("st,sd->td", dispatch, back, preferred_element_type=jnp.float32)
    gathered = gathered_all[:, :width]
    ffn_normed_grad = gathered_all[:, width:]
    layer_out = (hidden + gate[:, None] * gathered).astype(low)
    gate_grad = jnp.sum(upstream * gathered, axis=1)
    prob_grad = jnp.where(picked, gate_grad[:, None], 0.0)
    logit_grad = gate_probs * (prob_grad - jnp.sum(gate_probs * prob_grad, axis=1, keepdims=True))
    normed_wide = normed_ffn.astype(jnp.float32)
    router_grad = jnp.einsum("td,te->de", normed_wide, logit_grad, precision=highest)
    ffn_normed_grad = ffn_normed_grad + jnp.einsum(
        "te,de->td", logit_grad, full_router.astype(jnp.float32), precision=highest
    )
    norm_pull = jax.vjp(rms_norm, hidden, gain_ffn)[1]
    hidden_from_norm, gain_ffn_grad = norm_pull(ffn_normed_grad)
    hidden_grad = upstream + hidden_from_norm
    attn_grad = hidden_grad.astype(low)
    attn_out_grad = jnp.einsum("td,te->de", context, attn_grad, preferred_element_type=jnp.float32)
    context_grad = jnp.einsum("te,de->td", attn_grad, full_out, preferred_element_type=jnp.float32)
    context_grad = context_grad.astype(low).reshape(length, heads, head_size)
    prob_grad_attn = jnp.einsum(
        "qhc,khc->hqk", context_grad, values, preferred_element_type=jnp.float32
    )
    value_grad = jnp.einsum(
        "hqk,qhc->khc", probs_low, context_grad, preferred_element_type=jnp.float32
    )
    score_grad = probs * (prob_grad_attn - jnp.sum(probs * prob_grad_attn, axis=-1, keepdims=True))
    offset_grad = pairs_to_offsets(score_grad, length)
    table_grad = jnp.einsum("ho,ob->bh", offset_grad, offset_onehot, precision=highest)
    score_low = score_grad.astype(low)
    query_grad = (
        jnp.einsum("hqk,khc->qhc", score_low, keys, preferred_element_type=jnp.float32) * 0.125
    )
    key_grad = (
        jnp.einsum("hqk,qhc->khc", score_low, query, preferred_element_type=jnp.float32) * 0.125
    )
    projected_grad = jnp.stack(
        [
            query_grad.reshape(length, width),
            key_grad.reshape(length, width),
            value_grad.reshape(length, width),
        ]
    ).astype(low)
    attn_in_grad = jnp.einsum(
        "td,kte->kde", normed, projected_grad, preferred_element_type=jnp.float32
    )
    normed_grad = jnp.einsum(
        "kte,kde->td", projected_grad, full_in, preferred_element_type=jnp.float32
    )
    input_pull = jax.vjp(rms_norm, inputs, gain_attn)[1]
    input_from_norm, gain_attn_grad = input_pull(normed_grad)
    input_grad = hidden_grad + input_from_norm
    gains_grad = jnp.stack([gain_attn_grad, gain_ffn_grad])

    def spread(values):
        flat = values.astype(low).reshape(size, 1, -1)
        return jnp.pad(flat, ((0, 0), (0, 0), (0, width - flat.shape[2])))

    grads = jnp.concatenate(
        [
            jnp.transpose(attn_in_grad.astype(low).reshape(3, size, rows, width), (1, 0, 2, 3)).reshape(
                size, 3 * rows, width
            ),
            attn_out_grad.astype(low).reshape(size, rows, width),
            spread(jnp.transpose(gains_grad.reshape(2, size, rows), (1, 0, 2))),
            spread(router_grad),
            spread(table_grad),
            jnp.zeros((size, extra, width), low),
        ],
        axis=1,
    ).reshape(chips, 2, depth, width)
    kept = pick(grads, core, 1)
    given = swap(pick(grads, 1 - core, 1), size)
    kept = (kept.astype(jnp.float32) + given.astype(jnp.float32)).astype(low)
    mine = lax.psum_scatter(
        kept.reshape(chips * depth, width),
        "shard",
        scatter_dimension=0,
        tiled=True,
        axis_index_groups=groups,
    )
    mine = rep_sum(mine, reps)
    in_shard = mine[: 3 * rows].reshape(3, rows, width)
    out_shard = mine[3 * rows : 4 * rows]
    gains_shard = mine[spot, : 2 * rows].reshape(2, rows)
    router_shard = mine[spot + 1, : experts * rows].reshape(rows, experts)
    table_shard = mine[spot + 2, : table_rows * heads].reshape(table_rows, heads)
    return (
        layer_out,
        input_grad,
        in_shard,
        out_shard,
        gains_shard,
        router_shard,
        table_shard,
        expert_in_grad,
        expert_out_grad,
    )


def solution(mesh):
    placed = (
        P(("rep", "shard"), None),
        P(("rep", "shard"), None),
        P(("rep", "shard"), None),
        P(("rep", "shard"), None),
        P(),
        P(None, "shard", None),
        P("shard", None),
        P(None, "shard"),
        P("shard", None),
        P("shard", None),
        P(None, "shard", None),
        P(None, "shard", None),
    )
    return jax.shard_map(
        functools.partial(shards, mesh.shape["shard"], mesh.shape["rep"]),
        mesh=mesh,
        in_specs=placed,
        out_specs=(
            P(("rep", "shard"), None),
            P(("rep", "shard"), None),
            P(None, "shard", None),
            P("shard", None),
            P(None, "shard"),
            P("shard", None),
            P("shard", None),
            P(None, "shard", None),
            P(None, "shard", None),
        ),
        check_vma=False,
    )
```

```python
import functools

import jax
import jax.numpy as jnp
from jax import lax
from jax.experimental import pallas as pl
from jax.experimental.pallas import tpu as pltpu
from jax.sharding import PartitionSpec as P

BUCKETS = 32
CAP = 80


epsilon = 1e-06


def rms_norm(values, gain):
    return values * lax.rsqrt(jnp.mean(values * values, axis=-1, keepdims=True) + epsilon) * gain


def gelu_tanh(values):
    return jax.nn.gelu(values, approximate=True)


def offsets_to_pairs(per_offset, length):
    heads = per_offset.shape[0]
    reverse = per_offset[:, ::-1]
    repeated = jnp.broadcast_to(reverse[:, None, :], (heads, length, 2 * length - 1))
    repeated = repeated.reshape(heads, length * (2 * length - 1))
    repeated = jnp.pad(repeated, ((0, 0), (0, length)))
    skewed = repeated.reshape(heads, length, 2 * length)[:, :, :length]
    return skewed[:, :, ::-1]


def pairs_to_offsets(grid, length):
    heads = grid.shape[0]
    flipped = grid[:, :, ::-1]
    padded = jnp.pad(flipped, ((0, 0), (0, 0), (0, length)))
    flat = padded.reshape(heads, 2 * length * length)[:, : length * (2 * length - 1)]
    skewed = flat.reshape(heads, length, 2 * length - 1)
    return jnp.sum(skewed, axis=1)[:, ::-1]


def swap(array, size):
    return lax.ppermute(array, "shard", [(i, i ^ 1) for i in range(size)])


def pair_order(core, mine, other, axis):
    first = jnp.where(core == 0, mine, other)
    second = jnp.where(core == 0, other, mine)
    return jnp.concatenate([first, second], axis=axis)


def rep_sum(array, reps):
    if reps == 2:
        other = lax.ppermute(array, "rep", [(0, 1), (1, 0)])
        return array.astype(jnp.float32) + other.astype(jnp.float32)
    return lax.psum(array.astype(jnp.float32), "rep")


def pick(array, index, axis=0):
    return lax.dynamic_index_in_dim(array, index, axis, keepdims=False)


def pad_row(values, width):
    flat = values.reshape(-1)
    return jnp.pad(flat, (0, width - flat.shape[0])).reshape(1, width)


def grid_of(size):
    chips = size // 2
    outer = 4 if chips % 4 == 0 else 1
    return outer, chips // outer


def place_of(size):
    outer, inner = grid_of(size)
    me = lax.axis_index("shard")
    core = lax.rem(me, 2)
    chip = lax.div(me, 2)
    z = lax.div(chip, inner)
    y = lax.rem(chip, inner)

    def device(far, near):
        return {"shard": (far * inner + near) * 2 + core}

    return z, y, device


def greet(size):
    outer, inner = grid_of(size)
    z, y, device = place_of(size)
    barrier = pltpu.get_barrier_semaphore()
    for d in range(1, outer):
        pl.semaphore_signal(
            barrier,
            inc=1,
            device_id=device(lax.rem(z + d, outer), y),
            device_id_type=pl.DeviceIdType.MESH,
        )
    for e in range(1, inner):
        pl.semaphore_signal(
            barrier,
            inc=1,
            device_id=device(z, lax.rem(y + e, inner)),
            device_id_type=pl.DeviceIdType.MESH,
        )
    pl.semaphore_wait(barrier, outer + inner - 2)


def send(src, dst, send_sem, recv_sem, target):
    copy = pltpu.make_async_remote_copy(
        src_ref=src,
        dst_ref=dst,
        send_sem=send_sem,
        recv_sem=recv_sem,
        device_id=target,
        device_id_type=pl.DeviceIdType.MESH,
    )
    copy.start()
    return copy


def gather_kernel(size, x_ref, o_ref, own_sem, z_send, z_recv, y_send, y_recv):
    outer, inner = grid_of(size)
    z, y, device = place_of(size)
    chip = z * inner + y
    greet(size)
    own = pltpu.make_async_copy(x_ref, o_ref.at[chip], own_sem)
    own.start()
    along = []
    for d in range(1, outer):
        target = device(lax.rem(z + d, outer), y)
        along.append(send(x_ref, o_ref.at[chip], z_send.at[d - 1], z_recv.at[d - 1], target))
    across = []
    for e in range(1, inner):
        target = device(z, lax.rem(y + e, inner))
        across.append(send(x_ref, o_ref.at[chip], y_send.at[0, e - 1], y_recv.at[0, e - 1], target))
    for d in range(1, outer):
        along[d - 1].wait_recv()
        source = lax.rem(z + outer - d, outer) * inner + y
        for e in range(1, inner):
            target = device(z, lax.rem(y + e, inner))
            across.append(
                send(
                    o_ref.at[source],
                    o_ref.at[source],
                    y_send.at[d, e - 1],
                    y_recv.at[d, e - 1],
                    target,
                )
            )
    own.wait()
    for copy in across:
        copy.wait_recv()
    for copy in along + across:
        copy.wait_send()


def gather_chips(block, size, collective_id):
    outer, inner = grid_of(size)
    return pl.pallas_call(
        functools.partial(gather_kernel, size),
        out_shape=jax.ShapeDtypeStruct((size // 2,) + block.shape, block.dtype),
        in_specs=[pl.BlockSpec(memory_space=pltpu.VMEM)],
        out_specs=pl.BlockSpec(memory_space=pltpu.VMEM),
        scratch_shapes=[
            pltpu.SemaphoreType.DMA,
            pltpu.SemaphoreType.DMA((max(outer - 1, 1),)),
            pltpu.SemaphoreType.DMA((max(outer - 1, 1),)),
            pltpu.SemaphoreType.DMA((outer, max(inner - 1, 1))),
            pltpu.SemaphoreType.DMA((outer, max(inner - 1, 1))),
        ],
        compiler_params=pltpu.CompilerParams(
            collective_id=collective_id, has_side_effects=True, vmem_limit_bytes=40 << 20
        ),
    )(block)


def scatter_kernel(
    size, p_ref, o_ref, y_buf, z_out, z_in, total, y_send, y_recv, z_send, z_recv
):
    outer, inner = grid_of(size)
    z, y, device = place_of(size)
    rows = o_ref.shape[0]
    step = 16
    greet(size)
    across = {}
    order = [*range(1, outer), 0]
    for d in order:
        far = lax.rem(z + d, outer)
        for e in range(1, inner):
            near = lax.rem(y + e, inner)
            across[d, e] = send(
                p_ref.at[far * inner + near],
                y_buf.at[e - 1, d],
                y_send.at[d, e - 1],
                y_recv.at[d, e - 1],
                device(z, near),
            )
    along = []
    for d in order:
        far = lax.rem(z + d, outer)
        for e in range(1, inner):
            across[d, e].wait_recv()

        def add(i, carry):
            at = pl.ds(pl.multiple_of(i * step, step), step)
            value = p_ref[far * inner + y, at].astype(jnp.float32)
            for e in range(1, inner):
                value = value + y_buf[e - 1, d, at].astype(jnp.float32)
            if d == 0:
                total[at] = value
            else:
                z_out[d - 1, at] = value.astype(z_out.dtype)
            return carry

        lax.fori_loop(0, rows // step, add, 0)
        if d > 0:
            along.append(
                send(
                    z_out.at[d - 1],
                    z_in.at[d - 1],
                    z_send.at[d - 1],
                    z_recv.at[d - 1],
                    device(far, y),
                )
            )
    for copy in along:
        copy.wait_recv()

    def finish(i, carry):
        at = pl.ds(pl.multiple_of(i * step, step), step)
        value = total[at]
        for d in range(1, outer):
            value = value + z_in[d - 1, at].astype(jnp.float32)
        o_ref[at] = value.astype(o_ref.dtype)
        return carry

    lax.fori_loop(0, rows // step, finish, 0)
    for copy in [*along, *across.values()]:
        copy.wait_send()


def scatter_chips(partial, size, collective_id):
    outer, inner = grid_of(size)
    rows, width = partial.shape[1:]
    steps = max(outer - 1, 1)
    sides = max(inner - 1, 1)
    return pl.pallas_call(
        functools.partial(scatter_kernel, size),
        out_shape=jax.ShapeDtypeStruct((rows, width), partial.dtype),
        in_specs=[pl.BlockSpec(memory_space=pltpu.VMEM)],
        out_specs=pl.BlockSpec(memory_space=pltpu.VMEM),
        scratch_shapes=[
            pltpu.VMEM((sides, outer, rows, width), partial.dtype),
            pltpu.VMEM((steps, rows, width), partial.dtype),
            pltpu.VMEM((steps, rows, width), partial.dtype),
            pltpu.VMEM((rows, width), jnp.float32),
            pltpu.SemaphoreType.DMA((outer, sides)),
            pltpu.SemaphoreType.DMA((outer, sides)),
            pltpu.SemaphoreType.DMA((steps,)),
            pltpu.SemaphoreType.DMA((steps,)),
        ],
        compiler_params=pltpu.CompilerParams(
            collective_id=collective_id, has_side_effects=True, vmem_limit_bytes=48 << 20
        ),
    )(partial)


def shards(
    size,
    reps,
    tokens,
    cotangent,
    lengths,
    routes,
    bucket_ids,
    attn_in,
    attn_out,
    gains,
    router,
    rel_table,
    expert_in,
    expert_out,
):
    highest = lax.Precision.HIGHEST
    low = jnp.bfloat16
    length, width = tokens.shape
    heads = rel_table.shape[1]
    head_size = width // heads
    experts = expert_in.shape[0]
    capacity = CAP
    bucket_count = BUCKETS
    chips = size // 2
    rows = width // size
    hidden_units = expert_in.shape[2]
    strip = hidden_units // chips
    groups = [[2 * j + c for j in range(chips)] for c in range(2)]
    core = lax.axis_index("shard") % 2

    places = jnp.arange(length, dtype=jnp.int32)
    chosen = routes[:, 0]
    picked = chosen[:, None] == jnp.arange(experts, dtype=jnp.int32)[None, :]
    earlier = (places[None, :] < places[:, None]).astype(low)
    ranks = jnp.dot(earlier, picked.astype(low), preferred_element_type=jnp.float32)
    rank = jnp.sum(jnp.where(picked, ranks, 0.0), axis=1).astype(jnp.int32)
    slot = chosen * capacity + rank
    dispatch = (jnp.arange(experts * capacity, dtype=jnp.int32)[:, None] == slot[None, :]).astype(
        low
    )
    up_sent = jnp.dot(dispatch, cotangent, preferred_element_type=jnp.float32).astype(low)
    up_sent = up_sent.reshape(experts, capacity, width)
    up_mine = pick(up_sent, core)
    up_other = swap(pick(up_sent, 1 - core), size)
    up_block = jnp.concatenate([up_mine, up_other], axis=0)
    up_slots = lax.all_gather(up_block, "shard", axis=0, tiled=True, axis_index_groups=groups)

    packed = jnp.concatenate(
        [
            attn_in.reshape(3 * rows, width),
            attn_out,
            pad_row(gains, width),
            pad_row(router, width),
            pad_row(rel_table, width),
        ],
        axis=0,
    )
    depth = packed.shape[0]
    extra = -depth % 16
    packed = jnp.pad(packed, ((0, extra), (0, 0)))
    depth = depth + extra
    same = gather_chips(packed, size, 0)
    other = swap(same, size)
    whole = jnp.stack(
        [jnp.where(core == 0, same, other), jnp.where(core == 0, other, same)], axis=1
    ).reshape(size, depth, width)
    full_in = whole[:, : 3 * rows].reshape(size, 3, rows, width)
    full_in = jnp.transpose(full_in, (1, 0, 2, 3)).reshape(3, width, width)
    full_out = whole[:, 3 * rows : 4 * rows].reshape(width, width)
    spot = 4 * rows
    full_gains = whole[:, spot, : 2 * rows].reshape(size, 2, rows)
    full_gains = jnp.transpose(full_gains, (1, 0, 2)).reshape(2, width)
    full_router = whole[:, spot + 1, : experts * rows].reshape(width, experts)
    table_rows = bucket_count // size
    full_table = whole[:, spot + 2, : table_rows * heads].reshape(bucket_count, heads)

    in_mine = pick(expert_in, core)
    in_other = swap(pick(expert_in, 1 - core), size)
    in_rows = pair_order(core, in_mine, in_other, 0).reshape(2 * rows, chips, strip)
    in_rows = jnp.transpose(in_rows, (1, 0, 2))
    in_strip = lax.all_to_all(
        in_rows, "shard", 0, 0, axis_index_groups=groups, tiled=True
    ).reshape(width, strip)
    out_mine = pick(expert_out, core)
    out_other = swap(pick(expert_out, 1 - core), size)
    out_strip = pair_order(core, out_mine, out_other, 0)

    inputs = tokens.astype(jnp.float32)
    upstream = cotangent.astype(jnp.float32)
    gain_attn = full_gains[0].astype(jnp.float32)
    gain_ffn = full_gains[1].astype(jnp.float32)
    normed = rms_norm(inputs, gain_attn).astype(low)
    projected = jnp.einsum(
        "td,kde->kte", normed, full_in, preferred_element_type=jnp.float32
    ).astype(low)
    query = projected[0].reshape(length, heads, head_size)
    keys = projected[1].reshape(length, heads, head_size)
    values = projected[2].reshape(length, heads, head_size)
    offset_onehot = (
        bucket_ids[:, None] == jnp.arange(bucket_count, dtype=jnp.int32)[None, :]
    ).astype(jnp.float32)
    offset_bias = jnp.einsum(
        "ob,bh->ho", offset_onehot, full_table.astype(jnp.float32), precision=highest
    )
    bias = offsets_to_pairs(offset_bias, length)
    seqs = jnp.arange(lengths.shape[1], dtype=jnp.int32)
    ends = jnp.sum(jnp.where(seqs[None, :] <= seqs[:, None], lengths[0][None, :], 0), axis=1)
    segment = jnp.sum((places[:, None] >= ends[None, :]).astype(jnp.int32), axis=1)
    allowed = segment[:, None] == segment[None, :]
    raw = jnp.einsum("qhc,khc->hqk", query, keys, preferred_element_type=jnp.float32) * 0.125
    scores = jnp.where(allowed[None], raw + bias, -1e30)
    peak = jnp.max(scores, axis=-1, keepdims=True)
    expo = jnp.exp(scores - peak)
    totals = jnp.sum(expo, axis=-1, keepdims=True)
    probs = expo / totals
    probs_low = probs.astype(low)
    context = jnp.einsum("hqk,khc->qhc", probs_low, values, preferred_element_type=jnp.float32)
    context = context.astype(low).reshape(length, width)
    hidden = inputs + jnp.dot(context, full_out, preferred_element_type=jnp.float32)
    normed_ffn = rms_norm(hidden, gain_ffn).astype(low)
    logits = jnp.dot(normed_ffn, full_router, preferred_element_type=jnp.float32)
    gate_probs = jax.nn.softmax(logits, axis=-1)
    gate = jnp.sum(jnp.where(picked, gate_probs, 0.0), axis=1)
    sent = jnp.dot(dispatch, normed_ffn, preferred_element_type=jnp.float32).astype(low)
    sent = sent.reshape(experts, capacity, width)
    sent_mine = pick(sent, core)
    sent_other = swap(pick(sent, 1 - core), size)
    block = jnp.concatenate([sent_mine, sent_other], axis=0)
    batch = gather_chips(block, size, 1).reshape(2 * chips * capacity, width)
    slot_logits = jnp.dot(batch, full_router, preferred_element_type=jnp.float32)
    slot_gate = pick(jax.nn.softmax(slot_logits, axis=-1), core, 1)
    out_grad = (slot_gate[:, None] * up_slots.astype(jnp.float32)).astype(low)
    before = jnp.dot(batch, in_strip, preferred_element_type=jnp.float32)
    active_wide, pull = jax.vjp(gelu_tanh, before)
    active = active_wide.astype(low)
    returned = jnp.dot(active, out_strip, preferred_element_type=jnp.float32)
    active_grad = jnp.einsum("cd,fd->cf", out_grad, out_strip, preferred_element_type=jnp.float32)
    before_grad = pull(active_grad)[0].astype(low)
    batch_grad = jnp.einsum("cf,df->cd", before_grad, in_strip, preferred_element_type=jnp.float32)
    partial = jnp.concatenate([returned.astype(low), batch_grad.astype(low)], axis=1)
    summed = scatter_chips(partial.reshape(chips, 2 * capacity, 2 * width), size, 2)
    back_mine = summed[:capacity]
    back_other = swap(summed[capacity:], size)
    back = pair_order(core, back_mine, back_other, 0)

    in_grad = jnp.einsum("cd,cf->df", batch, before_grad, preferred_element_type=jnp.float32)
    outer_grad = jnp.einsum("cf,cd->fd", active, out_grad, preferred_element_type=jnp.float32)
    in_grad = lax.all_to_all(
        in_grad.astype(low).reshape(chips, 2 * rows, strip),
        "shard",
        0,
        0,
        axis_index_groups=groups,
        tiled=True,
    )
    in_grad = rep_sum(in_grad, reps)
    in_grad = jnp.transpose(in_grad, (1, 0, 2)).reshape(2, rows, hidden_units)
    grad_mine = pick(in_grad, core)
    grad_other = swap(pick(in_grad, 1 - core).astype(low), size).astype(jnp.float32)
    expert_in_grad = pair_order(core, grad_mine[None], grad_other[None], 0)
    outer_grad = rep_sum(outer_grad.astype(low), reps).reshape(2, strip // 2, width)
    outer_mine = pick(outer_grad, core)
    outer_other = swap(pick(outer_grad, 1 - core).astype(low), size).astype(jnp.float32)
    expert_out_grad = pair_order(core, outer_mine[None], outer_other[None], 0)

    gathered_all = jnp.einsum("st,sd->td", dispatch, back, preferred_element_type=jnp.float32)
    gathered = gathered_all[:, :width]
    ffn_normed_grad = gathered_all[:, width:]
    layer_out = (hidden + gate[:, None] * gathered).astype(low)
    gate_grad = jnp.sum(upstream * gathered, axis=1)
    prob_grad = jnp.where(picked, gate_grad[:, None], 0.0)
    logit_grad = gate_probs * (prob_grad - jnp.sum(gate_probs * prob_grad, axis=1, keepdims=True))
    normed_wide = normed_ffn.astype(jnp.float32)
    router_grad = jnp.einsum("td,te->de", normed_wide, logit_grad, precision=highest)
    ffn_normed_grad = ffn_normed_grad + jnp.einsum(
        "te,de->td", logit_grad, full_router.astype(jnp.float32), precision=highest
    )
    norm_pull = jax.vjp(rms_norm, hidden, gain_ffn)[1]
    hidden_from_norm, gain_ffn_grad = norm_pull(ffn_normed_grad)
    hidden_grad = upstream + hidden_from_norm
    attn_grad = hidden_grad.astype(low)
    attn_out_grad = jnp.einsum("td,te->de", context, attn_grad, preferred_element_type=jnp.float32)
    context_grad = jnp.einsum("te,de->td", attn_grad, full_out, preferred_element_type=jnp.float32)
    context_grad = context_grad.astype(low).reshape(length, heads, head_size)
    prob_grad_attn = jnp.einsum(
        "qhc,khc->hqk", context_grad, values, preferred_element_type=jnp.float32
    )
    value_grad = jnp.einsum(
        "hqk,qhc->khc", probs_low, context_grad, preferred_element_type=jnp.float32
    )
    score_grad = probs * (prob_grad_attn - jnp.sum(probs * prob_grad_attn, axis=-1, keepdims=True))
    offset_grad = pairs_to_offsets(score_grad, length)
    table_grad = jnp.einsum("ho,ob->bh", offset_grad, offset_onehot, precision=highest)
    score_low = score_grad.astype(low)
    query_grad = (
        jnp.einsum("hqk,khc->qhc", score_low, keys, preferred_element_type=jnp.float32) * 0.125
    )
    key_grad = (
        jnp.einsum("hqk,qhc->khc", score_low, query, preferred_element_type=jnp.float32) * 0.125
    )
    projected_grad = jnp.stack(
        [
            query_grad.reshape(length, width),
            key_grad.reshape(length, width),
            value_grad.reshape(length, width),
        ]
    ).astype(low)
    attn_in_grad = jnp.einsum(
        "td,kte->kde", normed, projected_grad, preferred_element_type=jnp.float32
    )
    normed_grad = jnp.einsum(
        "kte,kde->td", projected_grad, full_in, preferred_element_type=jnp.float32
    )
    input_pull = jax.vjp(rms_norm, inputs, gain_attn)[1]
    input_from_norm, gain_attn_grad = input_pull(normed_grad)
    input_grad = hidden_grad + input_from_norm
    gains_grad = jnp.stack([gain_attn_grad, gain_ffn_grad])

    def spread(values):
        flat = values.astype(low).reshape(size, 1, -1)
        return jnp.pad(flat, ((0, 0), (0, 0), (0, width - flat.shape[2])))

    grads = jnp.concatenate(
        [
            jnp.transpose(attn_in_grad.astype(low).reshape(3, size, rows, width), (1, 0, 2, 3)).reshape(
                size, 3 * rows, width
            ),
            attn_out_grad.astype(low).reshape(size, rows, width),
            spread(jnp.transpose(gains_grad.reshape(2, size, rows), (1, 0, 2))),
            spread(router_grad),
            spread(table_grad),
            jnp.zeros((size, extra, width), low),
        ],
        axis=1,
    ).reshape(chips, 2, depth, width)
    kept = pick(grads, core, 1)
    given = swap(pick(grads, 1 - core, 1), size)
    kept = (kept.astype(jnp.float32) + given.astype(jnp.float32)).astype(low)
    mine = scatter_chips(kept, size, 3)
    mine = rep_sum(mine, reps)
    in_shard = mine[: 3 * rows].reshape(3, rows, width)
    out_shard = mine[3 * rows : 4 * rows]
    gains_shard = mine[spot, : 2 * rows].reshape(2, rows)
    router_shard = mine[spot + 1, : experts * rows].reshape(rows, experts)
    table_shard = mine[spot + 2, : table_rows * heads].reshape(table_rows, heads)
    return (
        layer_out,
        input_grad,
        in_shard,
        out_shard,
        gains_shard,
        router_shard,
        table_shard,
        expert_in_grad,
        expert_out_grad,
    )


def solution(mesh):
    placed = (
        P(("rep", "shard"), None),
        P(("rep", "shard"), None),
        P(("rep", "shard"), None),
        P(("rep", "shard"), None),
        P(),
        P(None, "shard", None),
        P("shard", None),
        P(None, "shard"),
        P("shard", None),
        P("shard", None),
        P(None, "shard", None),
        P(None, "shard", None),
    )
    return jax.shard_map(
        functools.partial(shards, mesh.shape["shard"], mesh.shape["rep"]),
        mesh=mesh,
        in_specs=placed,
        out_specs=(
            P(("rep", "shard"), None),
            P(("rep", "shard"), None),
            P(None, "shard", None),
            P("shard", None),
            P(None, "shard"),
            P("shard", None),
            P("shard", None),
            P(None, "shard", None),
            P(None, "shard", None),
        ),
        check_vma=False,
    )
```

```python
import functools

import jax
import jax.numpy as jnp
from jax import lax
from jax.experimental import pallas as pl
from jax.experimental.pallas import tpu as pltpu
from jax.sharding import PartitionSpec as P

BUCKETS = 32
CAP = 80


epsilon = 1e-06


def rms_norm(values, gain):
    return values * lax.rsqrt(jnp.mean(values * values, axis=-1, keepdims=True) + epsilon) * gain


def gelu_tanh(values):
    return jax.nn.gelu(values, approximate=True)


def swap(array, size):
    return lax.ppermute(array, "shard", [(i, i ^ 1) for i in range(size)])


def pair_order(core, mine, other, axis):
    first = jnp.where(core == 0, mine, other)
    second = jnp.where(core == 0, other, mine)
    return jnp.concatenate([first, second], axis=axis)


def rep_sum(array, reps):
    if reps == 2:
        other = lax.ppermute(array, "rep", [(0, 1), (1, 0)])
        return array.astype(jnp.float32) + other.astype(jnp.float32)
    return lax.psum(array.astype(jnp.float32), "rep")


def pick(array, index, axis=0):
    return lax.dynamic_index_in_dim(array, index, axis, keepdims=False)


def pad_row(values, width):
    flat = values.reshape(-1)
    return jnp.pad(flat, (0, width - flat.shape[0])).reshape(1, width)


def grid_of(size):
    chips = size // 2
    outer = 4 if chips % 4 == 0 else 1
    return outer, chips // outer


def place_of(size):
    outer, inner = grid_of(size)
    me = lax.axis_index("shard")
    core = lax.rem(me, 2)
    chip = lax.div(me, 2)
    z = lax.div(chip, inner)
    y = lax.rem(chip, inner)

    def device(far, near):
        return {"shard": (far * inner + near) * 2 + core}

    return z, y, device


def greet(size):
    outer, inner = grid_of(size)
    z, y, device = place_of(size)
    barrier = pltpu.get_barrier_semaphore()
    for d in range(1, outer):
        pl.semaphore_signal(
            barrier,
            inc=1,
            device_id=device(lax.rem(z + d, outer), y),
            device_id_type=pl.DeviceIdType.MESH,
        )
    for e in range(1, inner):
        pl.semaphore_signal(
            barrier,
            inc=1,
            device_id=device(z, lax.rem(y + e, inner)),
            device_id_type=pl.DeviceIdType.MESH,
        )
    pl.semaphore_wait(barrier, outer + inner - 2)


def send(src, dst, send_sem, recv_sem, target):
    copy = pltpu.make_async_remote_copy(
        src_ref=src,
        dst_ref=dst,
        send_sem=send_sem,
        recv_sem=recv_sem,
        device_id=target,
        device_id_type=pl.DeviceIdType.MESH,
    )
    copy.start()
    return copy


def gather_kernel(size, x_ref, o_ref, own_sem, z_send, z_recv, y_send, y_recv):
    outer, inner = grid_of(size)
    z, y, device = place_of(size)
    chip = z * inner + y
    greet(size)
    own = pltpu.make_async_copy(x_ref, o_ref.at[chip], own_sem)
    own.start()
    along = []
    for d in range(1, outer):
        target = device(lax.rem(z + d, outer), y)
        along.append(send(x_ref, o_ref.at[chip], z_send.at[d - 1], z_recv.at[d - 1], target))
    across = []
    for e in range(1, inner):
        target = device(z, lax.rem(y + e, inner))
        across.append(send(x_ref, o_ref.at[chip], y_send.at[0, e - 1], y_recv.at[0, e - 1], target))
    for d in range(1, outer):
        along[d - 1].wait_recv()
        source = lax.rem(z + outer - d, outer) * inner + y
        for e in range(1, inner):
            target = device(z, lax.rem(y + e, inner))
            across.append(
                send(
                    o_ref.at[source],
                    o_ref.at[source],
                    y_send.at[d, e - 1],
                    y_recv.at[d, e - 1],
                    target,
                )
            )
    own.wait()
    for copy in across:
        copy.wait_recv()
    for copy in along + across:
        copy.wait_send()


def gather_chips(block, size, collective_id):
    outer, inner = grid_of(size)
    return pl.pallas_call(
        functools.partial(gather_kernel, size),
        out_shape=jax.ShapeDtypeStruct((size // 2,) + block.shape, block.dtype),
        in_specs=[pl.BlockSpec(memory_space=pltpu.VMEM)],
        out_specs=pl.BlockSpec(memory_space=pltpu.VMEM),
        scratch_shapes=[
            pltpu.SemaphoreType.DMA,
            pltpu.SemaphoreType.DMA((max(outer - 1, 1),)),
            pltpu.SemaphoreType.DMA((max(outer - 1, 1),)),
            pltpu.SemaphoreType.DMA((outer, max(inner - 1, 1))),
            pltpu.SemaphoreType.DMA((outer, max(inner - 1, 1))),
        ],
        compiler_params=pltpu.CompilerParams(
            collective_id=collective_id, has_side_effects=True, vmem_limit_bytes=40 << 20
        ),
    )(block)


def scatter_kernel(
    size, p_ref, o_ref, y_buf, z_out, z_in, total, y_send, y_recv, z_send, z_recv
):
    outer, inner = grid_of(size)
    z, y, device = place_of(size)
    rows = o_ref.shape[0]
    step = 16
    greet(size)
    across = {}
    order = [*range(1, outer), 0]
    for d in order:
        far = lax.rem(z + d, outer)
        for e in range(1, inner):
            near = lax.rem(y + e, inner)
            across[d, e] = send(
                p_ref.at[far * inner + near],
                y_buf.at[e - 1, d],
                y_send.at[d, e - 1],
                y_recv.at[d, e - 1],
                device(z, near),
            )
    along = []
    for d in order:
        far = lax.rem(z + d, outer)
        for e in range(1, inner):
            across[d, e].wait_recv()

        def add(i, carry):
            at = pl.ds(pl.multiple_of(i * step, step), step)
            value = p_ref[far * inner + y, at].astype(jnp.float32)
            for e in range(1, inner):
                value = value + y_buf[e - 1, d, at].astype(jnp.float32)
            if d == 0:
                total[at] = value
            else:
                z_out[d - 1, at] = value.astype(z_out.dtype)
            return carry

        lax.fori_loop(0, rows // step, add, 0)
        if d > 0:
            along.append(
                send(
                    z_out.at[d - 1],
                    z_in.at[d - 1],
                    z_send.at[d - 1],
                    z_recv.at[d - 1],
                    device(far, y),
                )
            )
    for copy in along:
        copy.wait_recv()

    def finish(i, carry):
        at = pl.ds(pl.multiple_of(i * step, step), step)
        value = total[at]
        for d in range(1, outer):
            value = value + z_in[d - 1, at].astype(jnp.float32)
        o_ref[at] = value.astype(o_ref.dtype)
        return carry

    lax.fori_loop(0, rows // step, finish, 0)
    for copy in [*along, *across.values()]:
        copy.wait_send()


def scatter_chips(partial, size, collective_id):
    outer, inner = grid_of(size)
    rows, width = partial.shape[1:]
    steps = max(outer - 1, 1)
    sides = max(inner - 1, 1)
    return pl.pallas_call(
        functools.partial(scatter_kernel, size),
        out_shape=jax.ShapeDtypeStruct((rows, width), partial.dtype),
        in_specs=[pl.BlockSpec(memory_space=pltpu.VMEM)],
        out_specs=pl.BlockSpec(memory_space=pltpu.VMEM),
        scratch_shapes=[
            pltpu.VMEM((sides, outer, rows, width), partial.dtype),
            pltpu.VMEM((steps, rows, width), partial.dtype),
            pltpu.VMEM((steps, rows, width), partial.dtype),
            pltpu.VMEM((rows, width), jnp.float32),
            pltpu.SemaphoreType.DMA((outer, sides)),
            pltpu.SemaphoreType.DMA((outer, sides)),
            pltpu.SemaphoreType.DMA((steps,)),
            pltpu.SemaphoreType.DMA((steps,)),
        ],
        compiler_params=pltpu.CompilerParams(
            collective_id=collective_id, has_side_effects=True, vmem_limit_bytes=48 << 20
        ),
    )(partial)


def attend_kernel(heads, head_size, p_ref, bias_ref, down_ref, across_ref, c_ref, probs_ref):
    length = p_ref.shape[1]
    allowed = down_ref[...] == across_ref[...]
    parts = []
    for h in range(heads):
        at = slice(h * head_size, (h + 1) * head_size)
        raw = lax.dot_general(
            p_ref[0, :, at],
            p_ref[1, :, at],
            (((1,), (1,)), ((), ())),
            preferred_element_type=jnp.float32,
        )
        spread = jnp.broadcast_to(bias_ref[h : h + 1, :], (length, 2 * length))
        skewed = pltpu.roll(spread, length + 1, 1, stride=1, stride_axis=0)
        scores = jnp.where(allowed, raw * 0.125 + skewed[:, :length], -1e30)
        expo = jnp.exp(scores - jnp.max(scores, axis=1, keepdims=True))
        probs = expo / jnp.sum(expo, axis=1, keepdims=True)
        probs_ref[h] = probs
        parts.append(
            jnp.dot(
                probs.astype(jnp.bfloat16), p_ref[2, :, at], preferred_element_type=jnp.float32
            )
        )
    c_ref[...] = jnp.concatenate(parts, axis=1).astype(c_ref.dtype)


def attend(projected, offset_bias, segment, heads):
    length, width = projected.shape[1:]
    return pl.pallas_call(
        functools.partial(attend_kernel, heads, width // heads),
        out_shape=(
            jax.ShapeDtypeStruct((length, width), jnp.bfloat16),
            jax.ShapeDtypeStruct((heads, length, length), jnp.float32),
        ),
        compiler_params=pltpu.CompilerParams(vmem_limit_bytes=32 << 20),
    )(projected, offset_bias, segment[:, None], segment[None, :])


def attend_back_kernel(heads, head_size, p_ref, probs_ref, g_ref, o_ref, diag_ref):
    length = p_ref.shape[1]
    row = lax.broadcasted_iota(jnp.int32, (length, length), 0)
    col = lax.broadcasted_iota(jnp.int32, (length, length), 1)
    mirror = jnp.where(row + col == length - 1, 1.0, 0.0).astype(jnp.bfloat16)
    blank = jnp.zeros((length, length), jnp.float32)
    down = (((0,), (0,)), ((), ()))
    parts = [[], [], []]
    for h in range(heads):
        at = slice(h * head_size, (h + 1) * head_size)
        grad = g_ref[:, at]
        probs = probs_ref[h]
        prob_grad = lax.dot_general(
            grad, p_ref[2, :, at], (((1,), (1,)), ((), ())), preferred_element_type=jnp.float32
        )
        total = jnp.sum(probs * prob_grad, axis=1, keepdims=True)
        low = (probs * (prob_grad - total)).astype(jnp.bfloat16)
        flipped = jnp.dot(low, mirror, preferred_element_type=jnp.float32)
        skewed = pltpu.roll(
            jnp.concatenate([flipped, blank], axis=1), 0, 1, stride=1, stride_axis=0
        )
        diag_ref[h : h + 1, :] = jnp.sum(skewed, axis=0, keepdims=True)
        parts[0].append(
            jnp.dot(low, p_ref[1, :, at], preferred_element_type=jnp.float32) * 0.125
        )
        parts[1].append(
            lax.dot_general(low, p_ref[0, :, at], down, preferred_element_type=jnp.float32) * 0.125
        )
        parts[2].append(
            lax.dot_general(
                probs.astype(jnp.bfloat16), grad, down, preferred_element_type=jnp.float32
            )
        )
    for k in range(3):
        o_ref[k] = jnp.concatenate(parts[k], axis=1).astype(o_ref.dtype)


def attend_back(projected, probs, context_grad):
    heads, length = probs.shape[:2]
    width = context_grad.shape[1]
    return pl.pallas_call(
        functools.partial(attend_back_kernel, heads, width // heads),
        out_shape=(
            jax.ShapeDtypeStruct((3, length, width), jnp.bfloat16),
            jax.ShapeDtypeStruct((heads, 2 * length), jnp.float32),
        ),
        compiler_params=pltpu.CompilerParams(vmem_limit_bytes=32 << 20),
    )(projected, probs, context_grad)


def shards(
    size,
    reps,
    tokens,
    cotangent,
    lengths,
    routes,
    bucket_ids,
    attn_in,
    attn_out,
    gains,
    router,
    rel_table,
    expert_in,
    expert_out,
):
    highest = lax.Precision.HIGHEST
    low = jnp.bfloat16
    length, width = tokens.shape
    heads = rel_table.shape[1]
    experts = expert_in.shape[0]
    capacity = CAP
    bucket_count = BUCKETS
    chips = size // 2
    rows = width // size
    hidden_units = expert_in.shape[2]
    strip = hidden_units // chips
    groups = [[2 * j + c for j in range(chips)] for c in range(2)]
    core = lax.axis_index("shard") % 2

    places = jnp.arange(length, dtype=jnp.int32)
    chosen = routes[:, 0]
    picked = chosen[:, None] == jnp.arange(experts, dtype=jnp.int32)[None, :]
    earlier = (places[None, :] < places[:, None]).astype(low)
    ranks = jnp.dot(earlier, picked.astype(low), preferred_element_type=jnp.float32)
    rank = jnp.sum(jnp.where(picked, ranks, 0.0), axis=1).astype(jnp.int32)
    slot = chosen * capacity + rank
    dispatch = (jnp.arange(experts * capacity, dtype=jnp.int32)[:, None] == slot[None, :]).astype(
        low
    )
    up_sent = jnp.dot(dispatch, cotangent, preferred_element_type=jnp.float32).astype(low)
    up_sent = up_sent.reshape(experts, capacity, width)
    up_mine = pick(up_sent, core)
    up_other = swap(pick(up_sent, 1 - core), size)
    up_block = jnp.concatenate([up_mine, up_other], axis=0)
    up_slots = lax.all_gather(up_block, "shard", axis=0, tiled=True, axis_index_groups=groups)

    packed = jnp.concatenate(
        [
            attn_in.reshape(3 * rows, width),
            attn_out,
            pad_row(gains, width),
            pad_row(router, width),
            pad_row(rel_table, width),
        ],
        axis=0,
    )
    depth = packed.shape[0]
    extra = -depth % 16
    packed = jnp.pad(packed, ((0, extra), (0, 0)))
    depth = depth + extra
    same = gather_chips(packed, size, 0)
    other = swap(same, size)
    whole = jnp.stack(
        [jnp.where(core == 0, same, other), jnp.where(core == 0, other, same)], axis=1
    ).reshape(size, depth, width)
    full_in = whole[:, : 3 * rows].reshape(size, 3, rows, width)
    full_in = jnp.transpose(full_in, (1, 0, 2, 3)).reshape(3, width, width)
    full_out = whole[:, 3 * rows : 4 * rows].reshape(width, width)
    spot = 4 * rows
    full_gains = whole[:, spot, : 2 * rows].reshape(size, 2, rows)
    full_gains = jnp.transpose(full_gains, (1, 0, 2)).reshape(2, width)
    full_router = whole[:, spot + 1, : experts * rows].reshape(width, experts)
    table_rows = bucket_count // size
    full_table = whole[:, spot + 2, : table_rows * heads].reshape(bucket_count, heads)

    in_mine = pick(expert_in, core)
    in_other = swap(pick(expert_in, 1 - core), size)
    in_rows = pair_order(core, in_mine, in_other, 0).reshape(2 * rows, chips, strip)
    in_rows = jnp.transpose(in_rows, (1, 0, 2))
    in_strip = lax.all_to_all(
        in_rows, "shard", 0, 0, axis_index_groups=groups, tiled=True
    ).reshape(width, strip)
    out_mine = pick(expert_out, core)
    out_other = swap(pick(expert_out, 1 - core), size)
    out_strip = pair_order(core, out_mine, out_other, 0)

    inputs = tokens.astype(jnp.float32)
    upstream = cotangent.astype(jnp.float32)
    gain_attn = full_gains[0].astype(jnp.float32)
    gain_ffn = full_gains[1].astype(jnp.float32)
    normed = rms_norm(inputs, gain_attn).astype(low)
    projected = jnp.einsum(
        "td,kde->kte", normed, full_in, preferred_element_type=jnp.float32
    ).astype(low)
    offset_onehot = (
        jnp.pad(bucket_ids, (0, 1), constant_values=-1)[:, None] == jnp.arange(bucket_count, dtype=jnp.int32)[None, :]
    ).astype(jnp.float32)
    offset_bias = jnp.einsum(
        "ob,bh->ho", offset_onehot, full_table.astype(jnp.float32), precision=highest
    )
    seqs = jnp.arange(lengths.shape[1], dtype=jnp.int32)
    ends = jnp.sum(jnp.where(seqs[None, :] <= seqs[:, None], lengths[0][None, :], 0), axis=1)
    segment = jnp.sum((places[:, None] >= ends[None, :]).astype(jnp.int32), axis=1)
    context, probs = attend(projected, offset_bias, segment, heads)
    hidden = inputs + jnp.dot(context, full_out, preferred_element_type=jnp.float32)
    normed_ffn = rms_norm(hidden, gain_ffn).astype(low)
    logits = jnp.dot(normed_ffn, full_router, preferred_element_type=jnp.float32)
    gate_probs = jax.nn.softmax(logits, axis=-1)
    gate = jnp.sum(jnp.where(picked, gate_probs, 0.0), axis=1)
    sent = jnp.dot(dispatch, normed_ffn, preferred_element_type=jnp.float32).astype(low)
    sent = sent.reshape(experts, capacity, width)
    sent_mine = pick(sent, core)
    sent_other = swap(pick(sent, 1 - core), size)
    block = jnp.concatenate([sent_mine, sent_other], axis=0)
    batch = gather_chips(block, size, 1).reshape(2 * chips * capacity, width)
    slot_logits = jnp.dot(batch, full_router, preferred_element_type=jnp.float32)
    slot_gate = pick(jax.nn.softmax(slot_logits, axis=-1), core, 1)
    out_grad = (slot_gate[:, None] * up_slots.astype(jnp.float32)).astype(low)
    before = jnp.dot(batch, in_strip, preferred_element_type=jnp.float32)
    active_wide, pull = jax.vjp(gelu_tanh, before)
    active = active_wide.astype(low)
    returned = jnp.dot(active, out_strip, preferred_element_type=jnp.float32)
    active_grad = jnp.einsum("cd,fd->cf", out_grad, out_strip, preferred_element_type=jnp.float32)
    before_grad = pull(active_grad)[0].astype(low)
    batch_grad = jnp.einsum("cf,df->cd", before_grad, in_strip, preferred_element_type=jnp.float32)
    partial = jnp.concatenate([returned.astype(low), batch_grad.astype(low)], axis=1)
    summed = scatter_chips(partial.reshape(chips, 2 * capacity, 2 * width), size, 2)
    back_mine = summed[:capacity]
    back_other = swap(summed[capacity:], size)
    back = pair_order(core, back_mine, back_other, 0)

    in_grad = jnp.einsum("cd,cf->df", batch, before_grad, preferred_element_type=jnp.float32)
    outer_grad = jnp.einsum("cf,cd->fd", active, out_grad, preferred_element_type=jnp.float32)
    in_grad = lax.all_to_all(
        in_grad.astype(low).reshape(chips, 2 * rows, strip),
        "shard",
        0,
        0,
        axis_index_groups=groups,
        tiled=True,
    )
    in_grad = rep_sum(in_grad, reps)
    in_grad = jnp.transpose(in_grad, (1, 0, 2)).reshape(2, rows, hidden_units)
    grad_mine = pick(in_grad, core)
    grad_other = swap(pick(in_grad, 1 - core).astype(low), size).astype(jnp.float32)
    expert_in_grad = pair_order(core, grad_mine[None], grad_other[None], 0)
    outer_grad = rep_sum(outer_grad.astype(low), reps).reshape(2, strip // 2, width)
    outer_mine = pick(outer_grad, core)
    outer_other = swap(pick(outer_grad, 1 - core).astype(low), size).astype(jnp.float32)
    expert_out_grad = pair_order(core, outer_mine[None], outer_other[None], 0)

    gathered_all = jnp.einsum("st,sd->td", dispatch, back, preferred_element_type=jnp.float32)
    gathered = gathered_all[:, :width]
    ffn_normed_grad = gathered_all[:, width:]
    layer_out = (hidden + gate[:, None] * gathered).astype(low)
    gate_grad = jnp.sum(upstream * gathered, axis=1)
    prob_grad = jnp.where(picked, gate_grad[:, None], 0.0)
    logit_grad = gate_probs * (prob_grad - jnp.sum(gate_probs * prob_grad, axis=1, keepdims=True))
    normed_wide = normed_ffn.astype(jnp.float32)
    router_grad = jnp.einsum("td,te->de", normed_wide, logit_grad, precision=highest)
    ffn_normed_grad = ffn_normed_grad + jnp.einsum(
        "te,de->td", logit_grad, full_router.astype(jnp.float32), precision=highest
    )
    norm_pull = jax.vjp(rms_norm, hidden, gain_ffn)[1]
    hidden_from_norm, gain_ffn_grad = norm_pull(ffn_normed_grad)
    hidden_grad = upstream + hidden_from_norm
    attn_grad = hidden_grad.astype(low)
    attn_out_grad = jnp.einsum("td,te->de", context, attn_grad, preferred_element_type=jnp.float32)
    context_grad = jnp.einsum("te,de->td", attn_grad, full_out, preferred_element_type=jnp.float32)
    context_grad = context_grad.astype(low)
    projected_grad, diagonal = attend_back(projected, probs, context_grad)
    offset_grad = diagonal[:, : 2 * length - 1][:, ::-1]
    table_grad = jnp.einsum(
        "ho,ob->bh", offset_grad, offset_onehot[: 2 * length - 1], precision=highest
    )
    attn_in_grad = jnp.einsum(
        "td,kte->kde", normed, projected_grad, preferred_element_type=jnp.float32
    )
    normed_grad = jnp.einsum(
        "kte,kde->td", projected_grad, full_in, preferred_element_type=jnp.float32
    )
    input_pull = jax.vjp(rms_norm, inputs, gain_attn)[1]
    input_from_norm, gain_attn_grad = input_pull(normed_grad)
    input_grad = hidden_grad + input_from_norm
    gains_grad = jnp.stack([gain_attn_grad, gain_ffn_grad])

    def spread(values):
        flat = values.reshape(size, 1, -1)
        return jnp.pad(flat, ((0, 0), (0, 0), (0, width - flat.shape[2])))

    small = jnp.concatenate(
        [
            spread(jnp.transpose(gains_grad.reshape(2, size, rows), (1, 0, 2))),
            spread(router_grad),
            spread(table_grad),
            jnp.zeros((size, extra, width), jnp.float32),
        ],
        axis=1,
    ).astype(low)
    attn_in_grad = attn_in_grad.astype(low).reshape(3, size, rows, width)
    grads = jnp.concatenate(
        [
            attn_in_grad[0],
            attn_in_grad[1],
            attn_in_grad[2],
            attn_out_grad.astype(low).reshape(size, rows, width),
            small,
        ],
        axis=1,
    ).reshape(chips, 2, depth, width)
    kept = pick(grads, core, 1)
    given = swap(pick(grads, 1 - core, 1), size)
    kept = (kept.astype(jnp.float32) + given.astype(jnp.float32)).astype(low)
    mine = scatter_chips(kept, size, 3)
    mine = rep_sum(mine, reps)
    in_shard = mine[: 3 * rows].reshape(3, rows, width)
    out_shard = mine[3 * rows : 4 * rows]
    gains_shard = mine[spot, : 2 * rows].reshape(2, rows)
    router_shard = mine[spot + 1, : experts * rows].reshape(rows, experts)
    table_shard = mine[spot + 2, : table_rows * heads].reshape(table_rows, heads)
    return (
        layer_out,
        input_grad,
        in_shard,
        out_shard,
        gains_shard,
        router_shard,
        table_shard,
        expert_in_grad,
        expert_out_grad,
    )


def solution(mesh):
    placed = (
        P(("rep", "shard"), None),
        P(("rep", "shard"), None),
        P(("rep", "shard"), None),
        P(("rep", "shard"), None),
        P(),
        P(None, "shard", None),
        P("shard", None),
        P(None, "shard"),
        P("shard", None),
        P("shard", None),
        P(None, "shard", None),
        P(None, "shard", None),
    )
    return jax.shard_map(
        functools.partial(shards, mesh.shape["shard"], mesh.shape["rep"]),
        mesh=mesh,
        in_specs=placed,
        out_specs=(
            P(("rep", "shard"), None),
            P(("rep", "shard"), None),
            P(None, "shard", None),
            P("shard", None),
            P(None, "shard"),
            P("shard", None),
            P("shard", None),
            P(None, "shard", None),
            P(None, "shard", None),
        ),
        check_vma=False,
    )
```
